512 devices in a mesh: major: 32 (over z_lo, y, core), minor: 16 (over z_hi, x).
Axes of the slice: x: 4, y: 4, z: 16 (z_hi: 4, z_lo: 4; z = z_hi * 4 + z_lo), core: 2. Of those that a mesh axis runs over, the one named last changes fastest.
Arguments:
- sequence_input: bfloat16 [4, 65536, 512], P(None, ('major', 'minor')), may hold values from -6 to 6
- first_depthwise_taps: float32 [3, 512], replicated, may hold values from -1 to 1
- first_norm_gain: float32 [512], replicated, may hold values from 0.5 to 1.5
- first_up_weight: bfloat16 [512, 1024], replicated, may hold values from -0.25 to 0.25
- first_down_weight: bfloat16 [1024, 512], replicated, may hold values from -0.1875 to 0.1875
- second_depthwise_taps: float32 [3, 512], replicated, may hold values from -1 to 1
- second_norm_gain: float32 [512], replicated, may hold values from 0.5 to 1.5
- second_up_weight: bfloat16 [512, 1024], replicated, may hold values from -0.25 to 0.25
- second_down_weight: bfloat16 [1024, 512], replicated, may hold values from -0.1875 to 0.1875
- pool_one: float32 [3, 512], replicated, may hold values from -1 to 1
- pool_two: float32 [3, 512], replicated, may hold values from -1 to 1
- pooled_cotangent: bfloat16 [4, 16384, 512], P(None, ('major', 'minor')), may hold values from -6 to 6
Outputs:
- pooled: bfloat16 [4, 16384, 512], P(None, ('major', 'minor'))
- input_grad: bfloat16 [4, 65536, 512], P(None, ('major', 'minor'))
The draws below stay inside these ranges and needn't reach their ends.
All inputs are finite; a program needn't handle non-finite values.
Results may differ from the reference program's by a relative error of at most 0.013.
Values may be sent and summed in bfloat16 or wider, within the bound.
A program may use at most 64 MiB of HBM per device.

```python
from functools import partial
import jax
import jax.numpy as jnp
from jax import lax

C = 512
HID = 1024
BATCH = 4
SEQ = 65536
FIRST_DILATION = 256
SECOND_DILATION = 1024


def level_of(rng, extent, pieces, least, largest):
    def one(axis_at, blocks):
        heights = jax.random.uniform(jax.random.fold_in(jax.random.fold_in(rng, 6), axis_at), (blocks,), jnp.float32, least / len(pieces), largest / len(pieces))
        return jnp.repeat(jnp.exp(heights), extent[axis_at] // blocks).reshape((-1,) + (1,) * (len(extent) - axis_at - 1))

    level = one(*pieces[0])
    for cut in pieces[1:]:
        level = level * one(*cut)
    return level


def bell_draw(stream_key, shape, deviation, reach, split=(), kind=jnp.bfloat16):
    factor_of = level_of(stream_key, shape, split, -0.22, 0.18) if split else 1.0
    drawn = jax.random.normal(stream_key, shape, jnp.float32) * deviation * factor_of
    return jnp.minimum(jnp.maximum(drawn, -reach), reach).astype(kind)


def setup_inputs(seed: int = 0) -> dict:
    seeds = jax.random.split(jax.random.key(seed), 13)
    return {
        "sequence_input": bell_draw(seeds[0], (BATCH, SEQ, C), 1.0, 6.0, ((1, 512),)),
        "first_depthwise_taps": jnp.clip(jax.random.uniform(seeds[1], (3, C), jnp.float32, -1.0, 1.0), -1.0, 1.0),
        "first_norm_gain": jnp.clip(jax.random.uniform(seeds[2], (C,), jnp.float32, 0.5, 1.5), 0.5, 1.5),
        "first_up_weight": bell_draw(seeds[3], (C, HID), C ** -0.5, 0.25),
        "first_down_weight": bell_draw(seeds[4], (HID, C), HID ** -0.5, 0.1875),
        "second_depthwise_taps": jnp.clip(jax.random.uniform(seeds[5], (3, C), jnp.float32, -1.0, 1.0), -1.0, 1.0),
        "second_norm_gain": jnp.clip(jax.random.uniform(seeds[6], (C,), jnp.float32, 0.5, 1.5), 0.5, 1.5),
        "second_up_weight": bell_draw(seeds[7], (C, HID), C ** -0.5, 0.25),
        "second_down_weight": bell_draw(seeds[8], (HID, C), HID ** -0.5, 0.1875),
        "pool_one": jnp.clip(jax.random.uniform(seeds[9], (3, C), jnp.float32, -1.0, 1.0), -1.0, 1.0),
        "pool_two": jnp.clip(jax.random.uniform(seeds[10], (3, C), jnp.float32, -1.0, 1.0), -1.0, 1.0),
        "pooled_cotangent": bell_draw(seeds[11], (BATCH, SEQ // 4, C), 1.0, 6.0, ((1, 512),)),
    }


def below(v, shift_len):
    return jnp.concatenate([jnp.zeros((shift_len, v.shape[1]), v.dtype), v[:-shift_len]], 0)

def above(v, shift_len):
    return jnp.concatenate([v[shift_len:], jnp.zeros((shift_len, v.shape[1]), v.dtype)], 0)

def block_forward(x, taps, gain, up, down, shift_len):
    xf = x.astype(jnp.float32)
    conv = taps[0] * below(xf, shift_len) + taps[1] * xf + taps[2] * above(xf, shift_len)
    scale = lax.rsqrt(lax.optimization_barrier(jnp.mean(conv * conv, -1, keepdims=True)) + 1e-06)
    normed = (conv * scale * gain).astype(jnp.bfloat16)
    hidden_pre = jnp.dot(normed, up, preferred_element_type=jnp.float32)
    hidden = jax.nn.gelu(hidden_pre, approximate=True).astype(jnp.bfloat16)
    out = (xf + jnp.dot(hidden, down, preferred_element_type=jnp.float32)).astype(jnp.bfloat16)
    return (out, conv, scale, hidden_pre)

def block_backward(grad_out, conv, scale, hidden_pre, taps, gain, up, down, shift_len):
    grad_b = grad_out.astype(jnp.bfloat16)
    grad_hidden = jnp.dot(grad_b, down.T, preferred_element_type=jnp.float32)
    pull = jax.vjp(partial(jax.nn.gelu, approximate=True), hidden_pre)[1]
    grad_pre = pull(grad_hidden)[0].astype(jnp.bfloat16)
    grad_norm = jnp.dot(grad_pre, up.T, preferred_element_type=jnp.float32)
    scaled = grad_norm * gain
    grad_conv = (scale * scaled - conv * (scale * scale * scale) * lax.optimization_barrier(jnp.mean(scaled * conv, -1, keepdims=True))).astype(jnp.bfloat16)
    gcf = grad_conv.astype(jnp.float32)
    return grad_out + taps[0] * above(gcf, shift_len) + taps[1] * gcf + taps[2] * below(gcf, shift_len)

def pool_rows(prev, even, odd, taps):
    return taps[0] * prev + taps[1] * even + taps[2] * odd

def pool_forward(v, taps):
    vf = v.astype(jnp.float32)
    even = vf[0::2]
    odd = vf[1::2]
    prev = jnp.concatenate([jnp.zeros((1, vf.shape[1]), jnp.float32), odd[:-1]], 0)
    return pool_rows(prev, even, odd, taps).astype(jnp.bfloat16)

def pool_backward(grad, taps):
    following = jnp.concatenate([grad[1:], jnp.zeros((1, grad.shape[1]), jnp.float32)], 0)
    even_part = taps[1] * grad
    odd_part = taps[2] * grad + taps[0] * following
    return jnp.stack([even_part, odd_part], 1).reshape(-1, grad.shape[1])

def reference(sequence_input, first_depthwise_taps, first_norm_gain, first_up_weight, first_down_weight, second_depthwise_taps, second_norm_gain, second_up_weight, second_down_weight, pool_one, pool_two, pooled_cotangent):
    block_list = ((first_depthwise_taps, first_norm_gain, first_up_weight, first_down_weight, FIRST_DILATION), (second_depthwise_taps, second_norm_gain, second_up_weight, second_down_weight, SECOND_DILATION))

    def window(pair):
        current, cotangent = pair
        saved = []
        for taps, gain, up, down, shift_len in block_list:
            current, conv, scale, hidden_pre = block_forward(current, taps, gain, up, down, shift_len)
            saved.append((conv, scale, hidden_pre))
        middle = pool_forward(current, pool_one)
        pooled = pool_forward(middle, pool_two)
        grad_mid = pool_backward(cotangent.astype(jnp.float32), pool_two)
        grad = pool_backward(grad_mid, pool_one)
        for index in (1, 0):
            taps, gain, up, down, shift_len = block_list[index]
            conv, scale, hidden_pre = saved[index]
            grad = block_backward(grad, conv, scale, hidden_pre, taps, gain, up, down, shift_len)
        return (pooled, grad.astype(jnp.bfloat16))
    return lax.map(window, (sequence_input, pooled_cotangent))
```

```python
import jax
import jax.numpy as jnp
from jax import lax
from jax.experimental import pallas as pl
from jax.experimental.pallas import tpu as pltpu
from jax.sharding import PartitionSpec as P

MESH = pl.DeviceIdType.MESH
F32 = jnp.float32
BF16 = jnp.bfloat16

C = 512
HID = 1024
MAJOR = 32
POS = 8
SUB = 4
ROWS = 16
CHUNK = SUB * ROWS
M = POS * ROWS
GELU_A = 0.7978845608028654
GELU_B = 0.044715


def dot(left, right):
    return jnp.dot(left, right, preferred_element_type=F32)


def one_hot(shape, match):
    row = lax.broadcasted_iota(jnp.int32, shape, 0)
    col = lax.broadcasted_iota(jnp.int32, shape, 1)
    return match(row, col).astype(F32).astype(BF16)


def rows_of(value):
    return value.reshape(-1, C)


def gelu_parts(a):
    square = a * a
    t = jnp.tanh(GELU_A * a * (1.0 + GELU_B * square))
    half = 0.5 + 0.5 * t
    slope = half + 0.5 * a * (1.0 - t * t) * (GELU_A * (1.0 + 3.0 * GELU_B * square))
    return a * half, slope


def kernel(
    x_ref, taps1, gain1, up1_hbm, down1_hbm, taps2, gain2, up2_hbm, down2_hbm, pool1, pool2, g_ref,
    pooled_ref, out_ref,
    xbuf, x1buf, gc2buf, gc1buf, gbuf, grimbuf, grim_a, grim_b, rimbuf, rim_a, rim_b,
    conv1, scale1, slope1, gy2, gy1, x2buf, obuf, pbuf, xsel, midb,
    up1, down1, up2, down2, up1t, down1t, up2t, down2t,
    xs, xr, gs, gr, hs, hr, os, orr, ps, pr, rs, rr, ws, loc,
):
    major, minor = lax.axis_index("major"), lax.axis_index("minor")
    zhi, x = minor // 4, minor % 4
    half, low = x // 2, x % 2
    me = zhi * 2 + half
    first, last = major == 0, major == MAJOR - 1
    head, tail = x == 0, x == 3

    def member(j):
        return (major, (j // 2) * 4 + (j % 2) * 2 + low)

    below, above = (major - 1, minor), (major + 1, minor)
    next_x = jnp.where(half == 0, x + 2, 1 - low)
    prev_x = jnp.where(half == 1, x - 2, 3 - low)
    follow, before = (major, zhi * 4 + next_x), (major, zhi * 4 + prev_x)
    over, under = (major + 1, zhi * 4), (major - 1, zhi * 4 + 3)
    side = (major, zhi * 4 + 3 - x)

    barrier = pltpu.get_barrier_semaphore()

    def greet(device):
        pl.semaphore_signal(barrier, inc=1, device_id=device, device_id_type=MESH)

    for step in range(1, POS):
        greet(member((me + step) % POS))
    greet(side)
    pl.when(jnp.logical_not(first))(lambda: greet(below))
    pl.when(jnp.logical_not(last))(lambda: greet(above))
    pl.when(jnp.logical_and(tail, jnp.logical_not(last)))(lambda: greet(over))
    pl.when(jnp.logical_and(head, jnp.logical_not(first)))(lambda: greet(under))

    weight_copies = [
        pltpu.make_async_copy(source, target, ws.at[k])
        for k, (source, target) in enumerate(
            ((up1_hbm, up1), (down1_hbm, down1), (up2_hbm, up2), (down2_hbm, down2))
        )
    ]
    for copy in weight_copies:
        copy.start()

    def remote(source, target, send, recv, device):
        return pltpu.make_async_remote_copy(
            src_ref=source, dst_ref=target, send_sem=send, recv_sem=recv,
            device_id=device, device_id_type=MESH,
        )

    def x_rows(j, s):
        return x_ref.at[j // 2, pl.ds((j % 2) * CHUNK + s * ROWS, ROWS)]

    def x_send(j, s):
        return remote(x_rows(j, s), xbuf.at[s, 1 + me], xs.at[s, j], xr.at[s, me], member(j))

    def x_recv(j, s):
        return remote(x_rows(j, s), xbuf.at[s, 1 + j], xs.at[s, j], xr.at[s, j], member(j))

    def x_local(s):
        return pltpu.make_async_copy(x_rows(me, s), xbuf.at[s, 1 + me], xr.at[s, me])

    def g_rows(j):
        return g_ref.at[j // 2, pl.ds((j % 2) * 16, 16)]

    def g_send(j):
        return remote(g_rows(j), gbuf.at[me], gs.at[j], gr.at[me], member(j))

    def g_recv(j):
        return remote(g_rows(j), gbuf.at[j], gs.at[j], gr.at[j], member(j))

    def g_local():
        return pltpu.make_async_copy(g_rows(me), gbuf.at[me], gr.at[me])

    def out_rows(s):
        return out_ref.at[zhi, pl.ds(half * CHUNK + s * ROWS, ROWS)]

    def o_send(j, s):
        return remote(obuf.at[s, j], out_rows(s), os.at[s, j], orr.at[s, me], member(j))

    def o_recv(j, s):
        rows = out_ref.at[j // 2, pl.ds((j % 2) * CHUNK + s * ROWS, ROWS)]
        return remote(obuf.at[s, j], rows, os.at[s, j], orr.at[s, j], member(j))

    def o_local(s):
        return pltpu.make_async_copy(obuf.at[s, me], out_rows(s), orr.at[s, me])

    def p_send(j):
        rows = pooled_ref.at[zhi, pl.ds(half * 16, 16)]
        return remote(pbuf.at[j], rows, ps.at[j], pr.at[me], member(j))

    def p_recv(j):
        rows = pooled_ref.at[j // 2, pl.ds((j % 2) * 16, 16)]
        return remote(pbuf.at[j], rows, ps.at[j], pr.at[j], member(j))

    def p_local():
        return pltpu.make_async_copy(pbuf.at[me], pooled_ref.at[zhi, pl.ds(half * 16, 16)], pr.at[me])

    def halo_down(kind, buf, reach, s):
        return remote(
            buf.at[s, pl.ds(reach, reach)], buf.at[s, pl.ds(reach + POS, reach)],
            hs.at[kind, s, 0], hr.at[kind, s, 0], below,
        )

    def halo_up(kind, buf, reach, s):
        return remote(
            buf.at[s, pl.ds(POS, reach)], buf.at[s, pl.ds(0, reach)],
            hs.at[kind, s, 1], hr.at[kind, s, 1], above,
        )

    def send_halos(kind, buf, reach, s):
        pl.when(jnp.logical_not(first))(lambda: halo_down(kind, buf, reach, s).start())
        pl.when(jnp.logical_not(last))(lambda: halo_up(kind, buf, reach, s).start())

    def wait_halos(kind, buf, reach, s):
        pl.when(jnp.logical_not(last))(lambda: halo_down(kind, buf, reach, s).wait_recv())
        pl.when(jnp.logical_not(first))(lambda: halo_up(kind, buf, reach, s).wait_recv())

    halos = ((xbuf, 1), (x1buf, 4), (gc2buf, 4), (gc1buf, 1))

    for buf, reach in halos:
        zeros = jnp.zeros((SUB, reach, ROWS, C), BF16)

        @pl.when(first)
        def _(buf=buf, reach=reach, zeros=zeros):
            buf[:, pl.ds(0, reach)] = zeros

        @pl.when(last)
        def _(buf=buf, reach=reach, zeros=zeros):
            buf[:, pl.ds(reach + POS, reach)] = zeros

    has_under = jnp.logical_and(head, jnp.logical_not(first))
    has_over = jnp.logical_and(tail, jnp.logical_not(last))

    @pl.when(jnp.logical_not(has_under))
    def _():
        rim_b[...] = jnp.zeros((16, C), BF16)

    @pl.when(jnp.logical_not(has_over))
    def _():
        grim_b[...] = jnp.zeros((16, C), BF16)

    partners = (
        POS
        + jnp.where(first, 0, 1) + jnp.where(last, 0, 1)
        + jnp.where(has_over, 1, 0) + jnp.where(has_under, 1, 0)
    )
    pl.semaphore_wait(barrier, partners)

    def send_x(s):
        for step in range(1, POS):
            x_send((me + step) % POS, s).start()
        x_local(s).start()

    send_x(0)
    send_x(1)
    for step in range(1, POS):
        g_send((me + step) % POS).start()
    g_local().start()
    send_x(2)
    send_x(3)

    for copy in weight_copies:
        copy.wait()
    up1t[...] = up1[...].T
    down1t[...] = down1[...].T
    up2t[...] = up2[...].T
    down2t[...] = down2[...].T

    def forward(buf, reach, s, taps, gain, up, down):
        lowered = rows_of(buf[s, pl.ds(0, POS)]).astype(F32)
        here = rows_of(buf[s, pl.ds(reach, POS)]).astype(F32)
        raised = rows_of(buf[s, pl.ds(2 * reach, POS)]).astype(F32)
        conv = taps[0:1] * lowered + taps[1:2] * here + taps[2:3] * raised
        scale = lax.rsqrt(jnp.mean(conv * conv, -1, keepdims=True) + 1e-06)
        normed = (conv * scale * gain[...]).astype(BF16)
        hidden, slope = gelu_parts(dot(normed, up[...]))
        out = (here + dot(hidden.astype(BF16), down[...])).astype(BF16)
        return out, conv, scale, slope

    def backward(grad, conv, scale, slope, gain, upt, downt):
        grad_pre = (slope * dot(grad.astype(BF16), downt[...])).astype(BF16)
        scaled = dot(grad_pre, upt[...]) * gain[...]
        mean = jnp.mean(scaled * conv, -1, keepdims=True)
        return (scale * scaled - conv * (scale * scale * scale) * mean).astype(BF16)

    def spread(grad, buf, reach, s, taps):
        lowered = rows_of(buf[s, pl.ds(0, POS)]).astype(F32)
        here = rows_of(buf[s, pl.ds(reach, POS)]).astype(F32)
        raised = rows_of(buf[s, pl.ds(2 * reach, POS)]).astype(F32)
        return grad + taps[0:1] * raised + taps[1:2] * here + taps[2:3] * lowered

    def top_coefficients():
        one, two = [pool1[k : k + 1] for k in range(3)], [pool2[k : k + 1] for k in range(3)]
        here = (one[1] * two[1], one[2] * two[1] + one[0] * two[2], one[1] * two[2], one[2] * two[2])
        ahead = (jnp.zeros((1, C), F32), one[0] * two[0], one[1] * two[0], one[2] * two[0] + one[0] * two[1])
        place = lax.broadcasted_iota(jnp.int32, (M, C), 0) % 4

        def pick(four):
            return jnp.where(place == 0, four[0], jnp.where(place == 1, four[1], jnp.where(place == 2, four[2], four[3])))

        return pick(here), pick(ahead)

    def stage_a(s):
        for step in range(1, POS):
            x_recv((me + step) % POS, s).wait_recv()
        x_local(s).wait()
        send_halos(0, xbuf, 1, s)

    def stage_b(s):
        wait_halos(0, xbuf, 1, s)
        out, conv, scale, slope = forward(xbuf, 1, s, taps1, gain1, up1, down1)
        x1buf[s, pl.ds(4, POS)] = out.reshape(POS, ROWS, C)
        send_halos(1, x1buf, 4, s)
        conv1[s] = conv
        scale1[s] = scale
        slope1[s] = slope

    def take_g():
        for step in range(1, POS):
            g_recv((me + step) % POS).wait_recv()
        g_local().wait()
        firsts = one_hot((16, M), lambda row, col: jnp.logical_and(col == row * 16, row < POS))
        grimbuf[...] = dot(firsts, rows_of(gbuf[...])).astype(BF16)
        remote(grimbuf, grim_a, rs.at[0], rr.at[0], before).start()
        pl.when(has_under)(lambda: remote(grimbuf, grim_b, rs.at[1], rr.at[1], under).start())

    def stage_c(s):
        pl.when(s == 0)(take_g)
        coef_here, coef_ahead = top_coefficients()
        g_all = rows_of(gbuf[...])

        def take(row, col, ahead):
            return jnp.logical_and(row // ROWS == col // 16, (row % ROWS) // 4 + ahead + 4 * s == col % 16)

        here = dot(one_hot((M, M), lambda row, col: take(row, col, 0)), g_all)
        ahead = dot(one_hot((M, M), lambda row, col: take(row, col, 1)), g_all)
        gy2[s] = coef_here * here + coef_ahead * ahead

        @pl.when(s == SUB - 1)
        def _():
            remote(grimbuf, grim_a, rs.at[0], rr.at[0], before).wait_recv()
            pl.when(has_over)(lambda: remote(grimbuf, grim_b, rs.at[1], rr.at[1], over).wait_recv())
            shift = jnp.where(tail, 1, 0)

            def from_a(row, col):
                return jnp.logical_and(row % ROWS >= ROWS - 4, jnp.logical_and(row // ROWS + shift == col, col < POS))

            def from_b(row, col):
                return jnp.logical_and(row >= M - 4, col == 0)

            rim = dot(one_hot((M, 16), from_a), grim_a[...]) + dot(one_hot((M, 16), from_b), grim_b[...])
            gy2[s] = gy2[s] + coef_ahead * rim

        wait_halos(1, x1buf, 4, s)
        out, conv, scale, slope = forward(x1buf, 4, s, taps2, gain2, up2, down2)
        x2buf[s] = out
        grad_conv = backward(gy2[s], conv, scale, slope, gain2, up2t, down2t)
        gc2buf[s, pl.ds(4, POS)] = grad_conv.reshape(POS, ROWS, C)
        send_halos(2, gc2buf, 4, s)

    def stage_d(s):
        wait_halos(2, gc2buf, 4, s)
        grad = spread(gy2[s], gc2buf, 4, s, taps2)
        grad_conv = backward(grad, conv1[s], scale1[s], slope1[s], gain1, up1t, down1t)
        gc1buf[s, pl.ds(1, POS)] = grad_conv.reshape(POS, ROWS, C)
        send_halos(3, gc1buf, 1, s)
        gy1[s] = grad

    def stage_e(s):
        wait_halos(3, gc1buf, 1, s)
        obuf[s] = spread(gy1[s], gc1buf, 1, s, taps1).astype(BF16).reshape(POS, ROWS, C)
        for step in range(1, POS):
            o_send((me + step) % POS, s).start()
        o_local(s).start()

    def pool_first():
        def pick(r):
            def match(row, col):
                j, place, bin_ = row % 16, col % M, col % ROWS
                return jnp.logical_and(
                    jnp.logical_and(row // 16 == place // ROWS, j // 4 == col // M), 4 * (j % 4) + r == bin_
                )

            return one_hot((M, SUB * M), match)

        x2_all = x2buf[...].reshape(SUB * M, C)
        for r in range(4):
            xsel[r] = dot(pick(r), x2_all)
        midb[...] = (pool1[0:1] * xsel[1] + pool1[1:2] * xsel[2] + pool1[2:3] * xsel[3]).astype(BF16)
        last_x = one_hot((16, M), lambda row, col: jnp.logical_and(col == row * 16 + 15, row < POS))
        last_m = one_hot((16, M), lambda row, col: col == (row - POS) * 16 + 15)
        rimbuf[...] = (dot(last_x, xsel[3].astype(BF16)) + dot(last_m, midb[...])).astype(BF16)
        remote(rimbuf, rim_a, rs.at[2], rr.at[2], follow).start()
        pl.when(has_over)(lambda: remote(rimbuf, rim_b, rs.at[3], rr.at[3], over).start())

    def pool_second():
        remote(rimbuf, rim_a, rs.at[2], rr.at[2], follow).wait_recv()
        pl.when(has_under)(lambda: remote(rimbuf, rim_b, rs.at[3], rr.at[3], under).wait_recv())
        shift = jnp.where(head, 1, 0)
        step_back = one_hot((M, M), lambda row, col: jnp.logical_and(row % 16 != 0, col == row - 1))

        def rim_of(base):
            def from_a(row, col):
                k = row // 16 - shift
                return jnp.logical_and(row % 16 == 0, jnp.logical_and(k >= 0, col == base + k))

            def from_b(row, col):
                return jnp.logical_and(row == 0, col == base + POS - 1)

            return dot(one_hot((M, 16), from_a), rim_a[...]) + dot(one_hot((M, 16), from_b), rim_b[...])

        x_back = dot(step_back, xsel[3].astype(BF16)) + rim_of(0)
        mid_back = dot(step_back, midb[...]) + rim_of(POS)
        mid_even = (pool1[0:1] * x_back + pool1[1:2] * xsel[0] + pool1[2:3] * xsel[1]).astype(BF16)
        pooled = pool2[0:1] * mid_back + pool2[1:2] * mid_even.astype(F32) + pool2[2:3] * midb[...].astype(F32)
        pbuf[...] = pooled.astype(BF16).reshape(POS, 16, C)
        for step in range(1, POS):
            p_send((me + step) % POS).start()
        p_local().start()

    def pipeline(t, carry):
        pl.when(t >= 4)(lambda: stage_e(t - 4))
        pl.when(jnp.logical_and(t >= 3, t < SUB + 3))(lambda: stage_d(t - 3))
        pl.when(jnp.logical_and(t >= 2, t < SUB + 2))(lambda: stage_c(t - 2))
        pl.when(jnp.logical_and(t >= 1, t < SUB + 1))(lambda: stage_b(t - 1))
        pl.when(t < SUB)(lambda: stage_a(t))
        pl.when(t == SUB + 1)(pool_first)
        pl.when(t == SUB + 2)(pool_second)
        return carry

    lax.fori_loop(0, SUB + 4, pipeline, 0)

    for step in range(1, POS):
        j = (me + step) % POS
        g_send(j).wait_send()
        p_send(j).wait_send()
        p_recv(j).wait_recv()
    p_local().wait()

    def drain(s, carry):
        for step in range(1, POS):
            j = (me + step) % POS
            x_send(j, s).wait_send()
            o_send(j, s).wait_send()
            o_recv(j, s).wait_recv()
        o_local(s).wait()
        for kind, (buf, reach) in enumerate(halos):
            pl.when(jnp.logical_not(first))(lambda: halo_down(kind, buf, reach, s).wait_send())
            pl.when(jnp.logical_not(last))(lambda: halo_up(kind, buf, reach, s).wait_send())
        return carry

    lax.fori_loop(0, SUB, drain, 0)
    remote(grimbuf, grim_a, rs.at[0], rr.at[0], before).wait_send()
    remote(rimbuf, rim_a, rs.at[2], rr.at[2], follow).wait_send()
    pl.when(has_under)(lambda: remote(grimbuf, grim_b, rs.at[1], rr.at[1], under).wait_send())
    pl.when(has_over)(lambda: remote(rimbuf, rim_b, rs.at[3], rr.at[3], over).wait_send())


def body(
    sequence_input, first_depthwise_taps, first_norm_gain, first_up_weight, first_down_weight,
    second_depthwise_taps, second_norm_gain, second_up_weight, second_down_weight,
    pool_one, pool_two, pooled_cotangent,
):
    whole = pl.BlockSpec(memory_space=pltpu.VMEM)
    there = pl.BlockSpec(memory_space=pl.ANY)
    dma = pltpu.SemaphoreType.DMA
    rim = pltpu.VMEM((16, C), BF16)
    return pl.pallas_call(
        kernel,
        out_shape=(
            jax.ShapeDtypeStruct(pooled_cotangent.shape, BF16),
            jax.ShapeDtypeStruct(sequence_input.shape, BF16),
        ),
        in_specs=[there, whole, whole, there, there, whole, whole, there, there, whole, whole, there],
        out_specs=(there, there),
        scratch_shapes=[
            pltpu.VMEM((SUB, POS + 2, ROWS, C), BF16),
            pltpu.VMEM((SUB, POS + 8, ROWS, C), BF16),
            pltpu.VMEM((SUB, POS + 8, ROWS, C), BF16),
            pltpu.VMEM((SUB, POS + 2, ROWS, C), BF16),
            pltpu.VMEM((POS, 16, C), BF16),
            rim, rim, rim, rim, rim, rim,
            pltpu.VMEM((SUB, M, C), F32),
            pltpu.VMEM((SUB, M, 1), F32),
            pltpu.VMEM((SUB, M, HID), F32),
            pltpu.VMEM((SUB, M, C), F32),
            pltpu.VMEM((SUB, M, C), F32),
            pltpu.VMEM((SUB, M, C), BF16),
            pltpu.VMEM((SUB, POS, ROWS, C), BF16),
            pltpu.VMEM((POS, 16, C), BF16),
            pltpu.VMEM((4, M, C), F32),
            pltpu.VMEM((M, C), BF16),
            pltpu.VMEM((C, HID), BF16), pltpu.VMEM((HID, C), BF16),
            pltpu.VMEM((C, HID), BF16), pltpu.VMEM((HID, C), BF16),
            pltpu.VMEM((HID, C), BF16), pltpu.VMEM((C, HID), BF16),
            pltpu.VMEM((HID, C), BF16), pltpu.VMEM((C, HID), BF16),
            dma((SUB, POS)), dma((SUB, POS)),
            dma((POS,)), dma((POS,)),
            dma((4, SUB, 2)), dma((4, SUB, 2)),
            dma((SUB, POS)), dma((SUB, POS)),
            dma((POS,)), dma((POS,)),
            dma((4,)), dma((4,)),
            dma((4,)), dma((1,)),
        ],
        compiler_params=pltpu.CompilerParams(
            collective_id=0, has_side_effects=True, vmem_limit_bytes=48 * 2**20
        ),
        cost_estimate=pl.CostEstimate(flops=4300000000, bytes_accessed=8000000, transcendentals=1000000),
    )(
        sequence_input, first_depthwise_taps, first_norm_gain.reshape(1, C), first_up_weight, first_down_weight,
        second_depthwise_taps, second_norm_gain.reshape(1, C), second_up_weight, second_down_weight,
        pool_one, pool_two, pooled_cotangent,
    )


def solution(mesh):
    split = P(None, ("major", "minor"), None)
    return jax.shard_map(
        body,
        mesh=mesh,
        in_specs=(split,) + (P(),) * 10 + (split,),
        out_specs=(split, split),
        check_vma=False,
    )
```

```python
import jax
import jax.numpy as jnp
from jax import lax
from jax.experimental import pallas as pl
from jax.experimental.pallas import tpu as pltpu
from jax.sharding import PartitionSpec as P

MESH = pl.DeviceIdType.MESH
F32 = jnp.float32
BF16 = jnp.bfloat16

C = 512
HID = 1024
MAJOR = 32
POS = 8
SUB = 4
ROWS = 16
CHUNK = SUB * ROWS
M = POS * ROWS
VMEM_BYTES = 60 * 2**20
GELU_A = 0.7978845608028654
GELU_B = 0.044715


def dot(left, right):
    return jnp.dot(left, right, preferred_element_type=F32)


def one_hot(shape, match):
    row = lax.broadcasted_iota(jnp.int32, shape, 0)
    col = lax.broadcasted_iota(jnp.int32, shape, 1)
    return match(row, col).astype(F32).astype(BF16)


def rows_of(value):
    return value.reshape(-1, C)


def gelu_parts(a):
    square = a * a
    t = jnp.tanh(GELU_A * a * (1.0 + GELU_B * square))
    half = 0.5 + 0.5 * t
    slope = half + 0.5 * a * (1.0 - t * t) * (GELU_A * (1.0 + 3.0 * GELU_B * square))
    return a * half, slope


def kernel(
    x_ref, taps1_hbm, gain1_hbm, up1_hbm, down1_hbm, taps2_hbm, gain2_hbm, up2_hbm, down2_hbm, pool1_hbm, pool2_hbm, g_ref,
    pooled_ref, out_ref,
    xbuf, x1buf, gc2buf, gc1buf, gbuf, grimbuf, grim_a, grim_b, rimbuf, rim_a, rim_b,
    conv1, scale1, slope1, gy2, gy1, x2buf, obuf, pbuf, xsel, midb,
    taps1, gain1, up1, down1, taps2, gain2, up2, down2, pool1, pool2, up1t, down1t, up2t, down2t,
    xs, xr, gs, gr, hs, hr, os, orr, ps, pr, rs, rr, ws,
):
    major, minor = lax.axis_index("major"), lax.axis_index("minor")
    zhi, x = minor // 4, minor % 4
    half, low = x // 2, x % 2
    me = zhi * 2 + half
    first, last = major == 0, major == MAJOR - 1
    head, tail = x == 0, x == 3

    def member(j):
        return (major, (j // 2) * 4 + (j % 2) * 2 + low)

    below, above = (major - 1, minor), (major + 1, minor)
    next_x = jnp.where(half == 0, x + 2, 1 - low)
    prev_x = jnp.where(half == 1, x - 2, 3 - low)
    follow, before = (major, zhi * 4 + next_x), (major, zhi * 4 + prev_x)
    over, under = (major + 1, zhi * 4), (major - 1, zhi * 4 + 3)
    side = (major, zhi * 4 + 3 - x)

    barrier = pltpu.get_barrier_semaphore()

    def greet(device):
        pl.semaphore_signal(barrier, inc=1, device_id=device, device_id_type=MESH)

    for step in range(1, POS):
        greet(member((me + step) % POS))
    greet(side)
    pl.when(jnp.logical_not(first))(lambda: greet(below))
    pl.when(jnp.logical_not(last))(lambda: greet(above))
    pl.when(jnp.logical_and(tail, jnp.logical_not(last)))(lambda: greet(over))
    pl.when(jnp.logical_and(head, jnp.logical_not(first)))(lambda: greet(under))

    parameter_copies = [
        pltpu.make_async_copy(source, target, ws.at[k])
        for k, (source, target) in enumerate(
            (
                (taps1_hbm, taps1), (gain1_hbm, gain1), (up1_hbm, up1), (down1_hbm, down1), (taps2_hbm, taps2),
                (gain2_hbm, gain2), (up2_hbm, up2), (down2_hbm, down2), (pool1_hbm, pool1), (pool2_hbm, pool2),
            )
        )
    ]
    for copy in parameter_copies:
        copy.start()

    def remote(source, target, send, recv, device):
        return pltpu.make_async_remote_copy(
            src_ref=source, dst_ref=target, send_sem=send, recv_sem=recv,
            device_id=device, device_id_type=MESH,
        )

    def x_rows(j, s):
        return x_ref.at[j // 2, pl.ds((j % 2) * CHUNK + s * ROWS, ROWS)]

    def x_send(j, s):
        return remote(x_rows(j, s), xbuf.at[s, 1 + me], xs.at[s, j], xr.at[s, me], member(j))

    def x_recv(j, s):
        return remote(x_rows(j, s), xbuf.at[s, 1 + j], xs.at[s, j], xr.at[s, j], member(j))

    def x_local(s):
        return pltpu.make_async_copy(x_rows(me, s), xbuf.at[s, 1 + me], xr.at[s, me])

    def g_rows(j):
        return g_ref.at[j // 2, pl.ds((j % 2) * 16, 16)]

    def g_send(j):
        return remote(g_rows(j), gbuf.at[me], gs.at[j], gr.at[me], member(j))

    def g_recv(j):
        return remote(g_rows(j), gbuf.at[j], gs.at[j], gr.at[j], member(j))

    def g_local():
        return pltpu.make_async_copy(g_rows(me), gbuf.at[me], gr.at[me])

    def out_rows(s):
        return out_ref.at[zhi, pl.ds(half * CHUNK + s * ROWS, ROWS)]

    def o_send(j, s):
        return remote(obuf.at[s, j], out_rows(s), os.at[s, j], orr.at[s, me], member(j))

    def o_recv(j, s):
        rows = out_ref.at[j // 2, pl.ds((j % 2) * CHUNK + s * ROWS, ROWS)]
        return remote(obuf.at[s, j], rows, os.at[s, j], orr.at[s, j], member(j))

    def o_local(s):
        return pltpu.make_async_copy(obuf.at[s, me], out_rows(s), orr.at[s, me])

    def p_send(j):
        rows = pooled_ref.at[zhi, pl.ds(half * 16, 16)]
        return remote(pbuf.at[j], rows, ps.at[j], pr.at[me], member(j))

    def p_recv(j):
        rows = pooled_ref.at[j // 2, pl.ds((j % 2) * 16, 16)]
        return remote(pbuf.at[j], rows, ps.at[j], pr.at[j], member(j))

    def p_local():
        return pltpu.make_async_copy(pbuf.at[me], pooled_ref.at[zhi, pl.ds(half * 16, 16)], pr.at[me])

    def halo_down(kind, buf, reach, s):
        return remote(
            buf.at[s, pl.ds(reach, reach)], buf.at[s, pl.ds(reach + POS, reach)],
            hs.at[kind, s, 0], hr.at[kind, s, 0], below,
        )

    def halo_up(kind, buf, reach, s):
        return remote(
            buf.at[s, pl.ds(POS, reach)], buf.at[s, pl.ds(0, reach)],
            hs.at[kind, s, 1], hr.at[kind, s, 1], above,
        )

    def send_halos(kind, buf, reach, s):
        pl.when(jnp.logical_not(first))(lambda: halo_down(kind, buf, reach, s).start())
        pl.when(jnp.logical_not(last))(lambda: halo_up(kind, buf, reach, s).start())

    def wait_halos(kind, buf, reach, s):
        pl.when(jnp.logical_not(last))(lambda: halo_down(kind, buf, reach, s).wait_recv())
        pl.when(jnp.logical_not(first))(lambda: halo_up(kind, buf, reach, s).wait_recv())

    halos = ((xbuf, 1), (x1buf, 4), (gc2buf, 4), (gc1buf, 1))

    for buf, reach in halos:
        zeros = jnp.zeros((SUB, reach, ROWS, C), BF16)

        @pl.when(first)
        def _(buf=buf, reach=reach, zeros=zeros):
            buf[:, pl.ds(0, reach)] = zeros

        @pl.when(last)
        def _(buf=buf, reach=reach, zeros=zeros):
            buf[:, pl.ds(reach + POS, reach)] = zeros

    has_under = jnp.logical_and(head, jnp.logical_not(first))
    has_over = jnp.logical_and(tail, jnp.logical_not(last))

    @pl.when(jnp.logical_not(has_under))
    def _():
        rim_b[...] = jnp.zeros((16, C), BF16)

    @pl.when(jnp.logical_not(has_over))
    def _():
        grim_b[...] = jnp.zeros((16, C), BF16)

    partners = (
        POS
        + jnp.where(first, 0, 1) + jnp.where(last, 0, 1)
        + jnp.where(has_over, 1, 0) + jnp.where(has_under, 1, 0)
    )
    pl.semaphore_wait(barrier, partners)

    def send_x(s):
        for step in range(1, POS):
            x_send((me + step) % POS, s).start()
        x_local(s).start()

    send_x(0)
    send_x(1)
    for step in range(1, POS):
        g_send((me + step) % POS).start()
    g_local().start()
    send_x(2)
    send_x(3)

    for copy in parameter_copies:
        copy.wait()
    up1t[...] = up1[...].T
    down1t[...] = down1[...].T
    up2t[...] = up2[...].T
    down2t[...] = down2[...].T

    def forward(buf, reach, s, taps, gain, up, down):
        lowered = rows_of(buf[s, pl.ds(0, POS)]).astype(F32)
        here = rows_of(buf[s, pl.ds(reach, POS)]).astype(F32)
        raised = rows_of(buf[s, pl.ds(2 * reach, POS)]).astype(F32)
        conv = taps[0:1] * lowered + taps[1:2] * here + taps[2:3] * raised
        scale = lax.rsqrt(jnp.mean(conv * conv, -1, keepdims=True) + 1e-06)
        normed = (conv * scale * gain[...]).astype(BF16)
        hidden, slope = gelu_parts(dot(normed, up[...]))
        out = (here + dot(hidden.astype(BF16), down[...])).astype(BF16)
        return out, conv, scale, slope

    def backward(grad, conv, scale, slope, gain, upt, downt):
        grad_pre = (slope * dot(grad.astype(BF16), downt[...])).astype(BF16)
        scaled = dot(grad_pre, upt[...]) * gain[...]
        mean = jnp.mean(scaled * conv, -1, keepdims=True)
        return (scale * scaled - conv * (scale * scale * scale) * mean).astype(BF16)

    def spread(grad, buf, reach, s, taps):
        lowered = rows_of(buf[s, pl.ds(0, POS)]).astype(F32)
        here = rows_of(buf[s, pl.ds(reach, POS)]).astype(F32)
        raised = rows_of(buf[s, pl.ds(2 * reach, POS)]).astype(F32)
        return grad + taps[0:1] * raised + taps[1:2] * here + taps[2:3] * lowered

    def top_coefficients():
        one, two = [pool1[k : k + 1] for k in range(3)], [pool2[k : k + 1] for k in range(3)]
        here = (one[1] * two[1], one[2] * two[1] + one[0] * two[2], one[1] * two[2], one[2] * two[2])
        ahead = (jnp.zeros((1, C), F32), one[0] * two[0], one[1] * two[0], one[2] * two[0] + one[0] * two[1])
        place = lax.broadcasted_iota(jnp.int32, (M, C), 0) % 4

        def pick(four):
            return jnp.where(place == 0, four[0], jnp.where(place == 1, four[1], jnp.where(place == 2, four[2], four[3])))

        return pick(here), pick(ahead)

    def stage_a(s):
        for step in range(1, POS):
            x_recv((me + step) % POS, s).wait_recv()
        x_local(s).wait()
        send_halos(0, xbuf, 1, s)

    def stage_b(s):
        wait_halos(0, xbuf, 1, s)
        out, conv, scale, slope = forward(xbuf, 1, s, taps1, gain1, up1, down1)
        x1buf[s, pl.ds(4, POS)] = out.reshape(POS, ROWS, C)
        send_halos(1, x1buf, 4, s)
        conv1[s] = conv
        scale1[s] = scale
        slope1[s] = slope

    def take_g():
        for step in range(1, POS):
            g_recv((me + step) % POS).wait_recv()
        g_local().wait()
        firsts = one_hot((16, M), lambda row, col: jnp.logical_and(col == row * 16, row < POS))
        grimbuf[...] = dot(firsts, rows_of(gbuf[...])).astype(BF16)
        remote(grimbuf, grim_a, rs.at[0], rr.at[0], before).start()
        pl.when(has_under)(lambda: remote(grimbuf, grim_b, rs.at[1], rr.at[1], under).start())

    def stage_c(s):
        pl.when(s == 0)(take_g)
        coef_here, coef_ahead = top_coefficients()
        g_all = rows_of(gbuf[...])

        def take(row, col, ahead):
            return jnp.logical_and(row // ROWS == col // 16, (row % ROWS) // 4 + ahead + 4 * s == col % 16)

        here = dot(one_hot((M, M), lambda row, col: take(row, col, 0)), g_all)
        ahead = dot(one_hot((M, M), lambda row, col: take(row, col, 1)), g_all)
        gy2[s] = coef_here * here + coef_ahead * ahead

        @pl.when(s == SUB - 1)
        def _():
            remote(grimbuf, grim_a, rs.at[0], rr.at[0], before).wait_recv()
            pl.when(has_over)(lambda: remote(grimbuf, grim_b, rs.at[1], rr.at[1], over).wait_recv())
            shift = jnp.where(tail, 1, 0)

            def from_a(row, col):
                return jnp.logical_and(row % ROWS >= ROWS - 4, jnp.logical_and(row // ROWS + shift == col, col < POS))

            def from_b(row, col):
                return jnp.logical_and(row >= M - 4, col == 0)

            rim = dot(one_hot((M, 16), from_a), grim_a[...]) + dot(one_hot((M, 16), from_b), grim_b[...])
            gy2[s] = gy2[s] + coef_ahead * rim

        wait_halos(1, x1buf, 4, s)
        out, conv, scale, slope = forward(x1buf, 4, s, taps2, gain2, up2, down2)
        x2buf[s] = out
        grad_conv = backward(gy2[s], conv, scale, slope, gain2, up2t, down2t)
        gc2buf[s, pl.ds(4, POS)] = grad_conv.reshape(POS, ROWS, C)
        send_halos(2, gc2buf, 4, s)

    def stage_d(s):
        wait_halos(2, gc2buf, 4, s)
        grad = spread(gy2[s], gc2buf, 4, s, taps2)
        grad_conv = backward(grad, conv1[s], scale1[s], slope1[s], gain1, up1t, down1t)
        gc1buf[s, pl.ds(1, POS)] = grad_conv.reshape(POS, ROWS, C)
        send_halos(3, gc1buf, 1, s)
        gy1[s] = grad

    def stage_e(s):
        wait_halos(3, gc1buf, 1, s)
        obuf[s] = spread(gy1[s], gc1buf, 1, s, taps1).astype(BF16).reshape(POS, ROWS, C)
        for step in range(1, POS):
            o_send((me + step) % POS, s).start()
        o_local(s).start()

    def pool_first():
        def pick(r):
            def match(row, col):
                j, place, bin_ = row % 16, col % M, col % ROWS
                return jnp.logical_and(
                    jnp.logical_and(row // 16 == place // ROWS, j // 4 == col // M), 4 * (j % 4) + r == bin_
                )

            return one_hot((M, SUB * M), match)

        x2_all = x2buf[...].reshape(SUB * M, C)
        for r in range(4):
            xsel[r] = dot(pick(r), x2_all)
        midb[...] = (pool1[0:1] * xsel[1] + pool1[1:2] * xsel[2] + pool1[2:3] * xsel[3]).astype(BF16)
        last_x = one_hot((16, M), lambda row, col: jnp.logical_and(col == row * 16 + 15, row < POS))
        last_m = one_hot((16, M), lambda row, col: col == (row - POS) * 16 + 15)
        rimbuf[...] = (dot(last_x, xsel[3].astype(BF16)) + dot(last_m, midb[...])).astype(BF16)
        remote(rimbuf, rim_a, rs.at[2], rr.at[2], follow).start()
        pl.when(has_over)(lambda: remote(rimbuf, rim_b, rs.at[3], rr.at[3], over).start())

    def pool_second():
        remote(rimbuf, rim_a, rs.at[2], rr.at[2], follow).wait_recv()
        pl.when(has_under)(lambda: remote(rimbuf, rim_b, rs.at[3], rr.at[3], under).wait_recv())
        shift = jnp.where(head, 1, 0)
        step_back = one_hot((M, M), lambda row, col: jnp.logical_and(row % 16 != 0, col == row - 1))

        def rim_of(base):
            def from_a(row, col):
                k = row // 16 - shift
                return jnp.logical_and(row % 16 == 0, jnp.logical_and(k >= 0, col == base + k))

            def from_b(row, col):
                return jnp.logical_and(row == 0, col == base + POS - 1)

            return dot(one_hot((M, 16), from_a), rim_a[...]) + dot(one_hot((M, 16), from_b), rim_b[...])

        x_back = dot(step_back, xsel[3].astype(BF16)) + rim_of(0)
        mid_back = dot(step_back, midb[...]) + rim_of(POS)
        mid_even = (pool1[0:1] * x_back + pool1[1:2] * xsel[0] + pool1[2:3] * xsel[1]).astype(BF16)
        pooled = pool2[0:1] * mid_back + pool2[1:2] * mid_even.astype(F32) + pool2[2:3] * midb[...].astype(F32)
        pbuf[...] = pooled.astype(BF16).reshape(POS, 16, C)
        for step in range(1, POS):
            p_send((me + step) % POS).start()
        p_local().start()

    def pipeline(t, carry):
        pl.when(t >= 4)(lambda: stage_e(t - 4))
        pl.when(jnp.logical_and(t >= 3, t < SUB + 3))(lambda: stage_d(t - 3))
        pl.when(jnp.logical_and(t >= 2, t < SUB + 2))(lambda: stage_c(t - 2))
        pl.when(jnp.logical_and(t >= 1, t < SUB + 1))(lambda: stage_b(t - 1))
        pl.when(t < SUB)(lambda: stage_a(t))
        pl.when(t == SUB + 1)(pool_first)
        pl.when(t == SUB + 2)(pool_second)
        return carry

    lax.fori_loop(0, SUB + 4, pipeline, 0)

    for step in range(1, POS):
        j = (me + step) % POS
        g_send(j).wait_send()
        p_send(j).wait_send()
        p_recv(j).wait_recv()
    p_local().wait()

    def drain(s, carry):
        for step in range(1, POS):
            j = (me + step) % POS
            x_send(j, s).wait_send()
            o_send(j, s).wait_send()
            o_recv(j, s).wait_recv()
        o_local(s).wait()
        for kind, (buf, reach) in enumerate(halos):
            pl.when(jnp.logical_not(first))(lambda: halo_down(kind, buf, reach, s).wait_send())
            pl.when(jnp.logical_not(last))(lambda: halo_up(kind, buf, reach, s).wait_send())
        return carry

    lax.fori_loop(0, SUB, drain, 0)
    remote(grimbuf, grim_a, rs.at[0], rr.at[0], before).wait_send()
    remote(rimbuf, rim_a, rs.at[2], rr.at[2], follow).wait_send()
    pl.when(has_under)(lambda: remote(grimbuf, grim_b, rs.at[1], rr.at[1], under).wait_send())
    pl.when(has_over)(lambda: remote(rimbuf, rim_b, rs.at[3], rr.at[3], over).wait_send())


def body(
    sequence_input, first_depthwise_taps, first_norm_gain, first_up_weight, first_down_weight,
    second_depthwise_taps, second_norm_gain, second_up_weight, second_down_weight,
    pool_one, pool_two, pooled_cotangent,
):
    there = pl.BlockSpec(memory_space=pl.ANY)
    dma = pltpu.SemaphoreType.DMA
    rim = pltpu.VMEM((16, C), BF16)
    three, one = pltpu.VMEM((3, C), F32), pltpu.VMEM((1, C), F32)
    return pl.pallas_call(
        kernel,
        out_shape=(
            jax.ShapeDtypeStruct(pooled_cotangent.shape, BF16),
            jax.ShapeDtypeStruct(sequence_input.shape, BF16),
        ),
        in_specs=[there] * 12,
        out_specs=(there, there),
        scratch_shapes=[
            pltpu.VMEM((SUB, POS + 2, ROWS, C), BF16),
            pltpu.VMEM((SUB, POS + 8, ROWS, C), BF16),
            pltpu.VMEM((SUB, POS + 8, ROWS, C), BF16),
            pltpu.VMEM((SUB, POS + 2, ROWS, C), BF16),
            pltpu.VMEM((POS, 16, C), BF16),
            rim, rim, rim, rim, rim, rim,
            pltpu.VMEM((SUB, M, C), F32),
            pltpu.VMEM((SUB, M, 1), F32),
            pltpu.VMEM((SUB, M, HID), F32),
            pltpu.VMEM((SUB, M, C), F32),
            pltpu.VMEM((SUB, M, C), F32),
            pltpu.VMEM((SUB, M, C), BF16),
            pltpu.VMEM((SUB, POS, ROWS, C), BF16),
            pltpu.VMEM((POS, 16, C), BF16),
            pltpu.VMEM((4, M, C), F32),
            pltpu.VMEM((M, C), BF16),
            three, one, pltpu.VMEM((C, HID), BF16), pltpu.VMEM((HID, C), BF16),
            three, one, pltpu.VMEM((C, HID), BF16), pltpu.VMEM((HID, C), BF16),
            three, three,
            pltpu.VMEM((HID, C), BF16), pltpu.VMEM((C, HID), BF16),
            pltpu.VMEM((HID, C), BF16), pltpu.VMEM((C, HID), BF16),
            dma((SUB, POS)), dma((SUB, POS)),
            dma((POS,)), dma((POS,)),
            dma((4, SUB, 2)), dma((4, SUB, 2)),
            dma((SUB, POS)), dma((SUB, POS)),
            dma((POS,)), dma((POS,)),
            dma((4,)), dma((4,)),
            dma((10,)),
        ],
        compiler_params=pltpu.CompilerParams(
            collective_id=0, has_side_effects=True, vmem_limit_bytes=VMEM_BYTES
        ),
        cost_estimate=pl.CostEstimate(flops=4300000000, bytes_accessed=8000000, transcendentals=1000000),
    )(
        sequence_input, first_depthwise_taps, first_norm_gain.reshape(1, C), first_up_weight, first_down_weight,
        second_depthwise_taps, second_norm_gain.reshape(1, C), second_up_weight, second_down_weight,
        pool_one, pool_two, pooled_cotangent,
    )


def solution(mesh):
    split = P(None, ("major", "minor"), None)
    return jax.shard_map(
        body,
        mesh=mesh,
        in_specs=(split,) + (P(),) * 10 + (split,),
        out_specs=(split, split),
        check_vma=False,
    )
```

```python
import jax
import jax.numpy as jnp
from jax import lax
from jax.experimental import pallas as pl
from jax.experimental.pallas import tpu as pltpu
from jax.sharding import PartitionSpec as P

MESH = pl.DeviceIdType.MESH
F32 = jnp.float32
BF16 = jnp.bfloat16

C = 512
HID = 1024
MAJOR = 32
POS = 8
SUB = 4
ROWS = 16
CHUNK = SUB * ROWS
M = POS * ROWS
REACH = 5
WIDE = POS + 2 * REACH
NEAR = POS + 2
MN = NEAR * ROWS
VMEM_BYTES = 60 * 2**20
GELU_A = 0.7978845608028654
GELU_B = 0.044715


def dot(left, right):
    return jnp.dot(left, right, preferred_element_type=F32)


def one_hot(shape, match):
    row = lax.broadcasted_iota(jnp.int32, shape, 0)
    col = lax.broadcasted_iota(jnp.int32, shape, 1)
    return match(row, col).astype(F32).astype(BF16)


def rows_of(value):
    return value.reshape(-1, C)


def gelu_tanh(a):
    return jnp.tanh(GELU_A * a * (1.0 + GELU_B * (a * a)))


def gelu_slope(a, t):
    return 0.5 + 0.5 * t + 0.5 * a * (1.0 - t * t) * (GELU_A * (1.0 + 3.0 * GELU_B * (a * a)))


def kernel(
    x_ref, taps1_hbm, gain1_hbm, up1_hbm, down1_hbm, taps2_hbm, gain2_hbm, up2_hbm, down2_hbm, pool1_hbm, pool2_hbm, g_ref,
    pooled_ref, out_ref,
    xbuf, x1buf, gc2buf, gc1buf, gbuf, grimbuf, grim_a, grim_b, rimbuf, rim_a, rim_b,
    conv1, scale1, slope1, gy2, x2buf, obuf, pbuf, xsel, midb,
    taps1, gain1, up1, down1, taps2, gain2, up2, down2, pool1, pool2, up1t, down1t, up2t, down2t,
    xs, xr, gs, gr, hs, hr, os, orr, ps, pr, rs, rr, ws,
):
    major, minor = lax.axis_index("major"), lax.axis_index("minor")
    zhi, x = minor // 4, minor % 4
    half, low = x // 2, x % 2
    me = zhi * 2 + half
    first, last = major == 0, major == MAJOR - 1
    head, tail = x == 0, x == 3

    def member(j):
        return (major, (j // 2) * 4 + (j % 2) * 2 + low)

    below, above = (major - 1, minor), (major + 1, minor)
    next_x = jnp.where(half == 0, x + 2, 1 - low)
    prev_x = jnp.where(half == 1, x - 2, 3 - low)
    follow, before = (major, zhi * 4 + next_x), (major, zhi * 4 + prev_x)
    over, under = (major + 1, zhi * 4), (major - 1, zhi * 4 + 3)
    side = (major, zhi * 4 + 3 - x)

    barrier = pltpu.get_barrier_semaphore()

    def greet(device):
        pl.semaphore_signal(barrier, inc=1, device_id=device, device_id_type=MESH)

    for step in range(1, POS):
        greet(member((me + step) % POS))
    greet(side)
    pl.when(jnp.logical_not(first))(lambda: greet(below))
    pl.when(jnp.logical_not(last))(lambda: greet(above))
    pl.when(jnp.logical_and(tail, jnp.logical_not(last)))(lambda: greet(over))
    pl.when(jnp.logical_and(head, jnp.logical_not(first)))(lambda: greet(under))

    parameter_copies = [
        pltpu.make_async_copy(source, target, ws.at[k])
        for k, (source, target) in enumerate(
            (
                (taps1_hbm, taps1), (gain1_hbm, gain1), (up1_hbm, up1), (down1_hbm, down1), (taps2_hbm, taps2),
                (gain2_hbm, gain2), (up2_hbm, up2), (down2_hbm, down2), (pool1_hbm, pool1), (pool2_hbm, pool2),
            )
        )
    ]
    for copy in parameter_copies:
        copy.start()

    def remote(source, target, send, recv, device):
        return pltpu.make_async_remote_copy(
            src_ref=source, dst_ref=target, send_sem=send, recv_sem=recv,
            device_id=device, device_id_type=MESH,
        )

    def x_rows(j, s):
        return x_ref.at[j // 2, pl.ds((j % 2) * CHUNK + s * ROWS, ROWS)]

    def x_send(j, s):
        return remote(x_rows(j, s), xbuf.at[s, REACH + me], xs.at[s, j], xr.at[s, me], member(j))

    def x_recv(j, s):
        return remote(x_rows(j, s), xbuf.at[s, REACH + j], xs.at[s, j], xr.at[s, j], member(j))

    def x_local(s):
        return pltpu.make_async_copy(x_rows(me, s), xbuf.at[s, REACH + me], xr.at[s, me])

    def g_rows(j):
        return g_ref.at[j // 2, pl.ds((j % 2) * 16, 16)]

    def g_send(j):
        return remote(g_rows(j), gbuf.at[1 + me], gs.at[j], gr.at[me], member(j))

    def g_recv(j):
        return remote(g_rows(j), gbuf.at[1 + j], gs.at[j], gr.at[j], member(j))

    def g_local():
        return pltpu.make_async_copy(g_rows(me), gbuf.at[1 + me], gr.at[me])

    def out_rows(s):
        return out_ref.at[zhi, pl.ds(half * CHUNK + s * ROWS, ROWS)]

    def o_send(j, s):
        return remote(obuf.at[s, j], out_rows(s), os.at[s, j], orr.at[s, me], member(j))

    def o_recv(j, s):
        rows = out_ref.at[j // 2, pl.ds((j % 2) * CHUNK + s * ROWS, ROWS)]
        return remote(obuf.at[s, j], rows, os.at[s, j], orr.at[s, j], member(j))

    def o_local(s):
        return pltpu.make_async_copy(obuf.at[s, me], out_rows(s), orr.at[s, me])

    def p_send(j):
        rows = pooled_ref.at[zhi, pl.ds(half * 16, 16)]
        return remote(pbuf.at[j], rows, ps.at[j], pr.at[me], member(j))

    def p_recv(j):
        rows = pooled_ref.at[j // 2, pl.ds((j % 2) * 16, 16)]
        return remote(pbuf.at[j], rows, ps.at[j], pr.at[j], member(j))

    def p_local():
        return pltpu.make_async_copy(pbuf.at[me], pooled_ref.at[zhi, pl.ds(half * 16, 16)], pr.at[me])

    def halo_down(kind, buf, reach, s):
        return remote(
            buf.at[pl.ds(reach, reach)], buf.at[pl.ds(reach + POS, reach)],
            hs.at[kind, s, 0], hr.at[kind, s, 0], below,
        )

    def halo_up(kind, buf, reach, s):
        return remote(
            buf.at[pl.ds(POS, reach)], buf.at[pl.ds(0, reach)], hs.at[kind, s, 1], hr.at[kind, s, 1], above,
        )

    def send_halos(kind, buf, reach, s):
        pl.when(jnp.logical_not(first))(lambda: halo_down(kind, buf, reach, s).start())
        pl.when(jnp.logical_not(last))(lambda: halo_up(kind, buf, reach, s).start())

    def wait_halos(kind, buf, reach, s):
        pl.when(jnp.logical_not(last))(lambda: halo_down(kind, buf, reach, s).wait_recv())
        pl.when(jnp.logical_not(first))(lambda: halo_up(kind, buf, reach, s).wait_recv())

    def end_halos(kind, buf, reach, s):
        pl.when(jnp.logical_not(first))(lambda: halo_down(kind, buf, reach, s).wait_send())
        pl.when(jnp.logical_not(last))(lambda: halo_up(kind, buf, reach, s).wait_send())

    zeros = jnp.zeros((SUB, REACH, ROWS, C), BF16)

    @pl.when(first)
    def _():
        xbuf[:, pl.ds(0, REACH)] = zeros
        gc2buf[:, pl.ds(0, REACH)] = zeros
        gbuf[0] = zeros[0, 0]

    @pl.when(last)
    def _():
        xbuf[:, pl.ds(REACH + POS, REACH)] = zeros
        gc2buf[:, pl.ds(REACH + POS, REACH)] = zeros
        gbuf[1 + POS] = zeros[0, 0]

    has_under = jnp.logical_and(head, jnp.logical_not(first))
    has_over = jnp.logical_and(tail, jnp.logical_not(last))

    @pl.when(jnp.logical_not(has_under))
    def _():
        rim_b[...] = jnp.zeros((16, C), BF16)

    @pl.when(jnp.logical_not(has_over))
    def _():
        grim_b[...] = jnp.zeros((16, C), BF16)

    partners = (
        POS
        + jnp.where(first, 0, 1) + jnp.where(last, 0, 1)
        + jnp.where(has_over, 1, 0) + jnp.where(has_under, 1, 0)
    )
    pl.semaphore_wait(barrier, partners)

    def send_x(s):
        for step in range(1, POS):
            x_send((me + step) % POS, s).start()
        x_local(s).start()

    def send_g():
        for step in range(1, POS):
            g_send((me + step) % POS).start()
        g_local().start()

    send_x(0)
    send_x(1)
    send_g()
    send_x(2)
    send_x(3)

    for copy in parameter_copies:
        copy.wait()
    up1t[...] = up1[...].T
    down1t[...] = down1[...].T
    up2t[...] = up2[...].T
    down2t[...] = down2[...].T

    def three_of(buf, reach, count):
        return [rows_of(buf[pl.ds(k * reach, count)]).astype(F32) for k in range(3)]

    def forward(buf, reach, count, taps, gain, up, down):
        lowered, here, raised = three_of(buf, reach, count)
        conv = taps[0:1] * lowered + taps[1:2] * here + taps[2:3] * raised
        scale = lax.rsqrt(jnp.mean(conv * conv, -1, keepdims=True) + 1e-06)
        normed = (conv * scale * gain[...]).astype(BF16)
        a = dot(normed, up[...])
        t = gelu_tanh(a)
        hidden = (a * (0.5 + 0.5 * t)).astype(BF16)
        out = (here + dot(hidden, down[...])).astype(BF16)
        return out, conv, scale, a, t

    def backward(grad, conv, scale, slope, gain, upt, downt):
        grad_pre = (slope * dot(grad.astype(BF16), downt[...])).astype(BF16)
        scaled = dot(grad_pre, upt[...]) * gain[...]
        mean = jnp.mean(scaled * conv, -1, keepdims=True)
        return (scale * scaled - conv * (scale * scale * scale) * mean).astype(BF16)

    def spread(grad, buf, reach, count, taps):
        lowered, here, raised = three_of(buf, reach, count)
        return grad + taps[0:1] * raised + taps[1:2] * here + taps[2:3] * lowered

    def top_coefficients(rows):
        one, two = [pool1[k : k + 1] for k in range(3)], [pool2[k : k + 1] for k in range(3)]
        here = (one[1] * two[1], one[2] * two[1] + one[0] * two[2], one[1] * two[2], one[2] * two[2])
        ahead = (jnp.zeros((1, C), F32), one[0] * two[0], one[1] * two[0], one[2] * two[0] + one[0] * two[1])
        place = lax.broadcasted_iota(jnp.int32, (rows, C), 0) % 4

        def pick(four):
            return jnp.where(place == 0, four[0], jnp.where(place == 1, four[1], jnp.where(place == 2, four[2], four[3])))

        return pick(here), pick(ahead)

    def take_g():
        for step in range(1, POS):
            g_recv((me + step) % POS).wait_recv()
        g_local().wait()
        send_halos(2, gbuf, 1, 0)

    def share_g():
        wait_halos(2, gbuf, 1, 0)
        firsts = one_hot((16, MN), lambda row, col: jnp.logical_and(col == row * 16, row < NEAR))
        grimbuf[...] = dot(firsts, rows_of(gbuf[...])).astype(BF16)
        remote(grimbuf, grim_a, rs.at[0], rr.at[0], before).start()
        pl.when(has_under)(lambda: remote(grimbuf, grim_b, rs.at[1], rr.at[1], under).start())

    def take_g_rims():
        remote(grimbuf, grim_a, rs.at[0], rr.at[0], before).wait_recv()
        pl.when(has_over)(lambda: remote(grimbuf, grim_b, rs.at[1], rr.at[1], over).wait_recv())

    def grad_top(s, start, count):
        rows = count * ROWS
        place = pl.ds(start * ROWS, rows)
        coef_here, coef_ahead = top_coefficients(rows)
        g_all = rows_of(gbuf[pl.ds(start, count)])

        def take(row, col, ahead):
            return jnp.logical_and(row // ROWS == col // 16, (row % ROWS) // 4 + ahead + 4 * s == col % 16)

        here = dot(one_hot((rows, rows), lambda row, col: take(row, col, 0)), g_all)
        ahead = dot(one_hot((rows, rows), lambda row, col: take(row, col, 1)), g_all)
        gy2[place] = coef_here * here + coef_ahead * ahead

        @pl.when(s == SUB - 1)
        def _():
            shift = jnp.where(tail, 1, 0)

            def end(row):
                return row % ROWS >= ROWS - 4

            def from_a(row, col):
                return jnp.logical_and(end(row), jnp.logical_and(row // ROWS + start + shift == col, col < NEAR))

            def from_b(row, col):
                return jnp.logical_and(end(row), jnp.logical_and(row // ROWS + start == NEAR - 1, col == 2))

            rim = dot(one_hot((rows, 16), from_a), grim_a[...]) + dot(one_hot((rows, 16), from_b), grim_b[...])
            gy2[place] = gy2[place] + coef_ahead * rim

    def stage_a(s):
        for step in range(1, POS):
            x_recv((me + step) % POS, s).wait_recv()
        x_local(s).wait()
        send_halos(0, xbuf.at[s], REACH, s)

    def stage_b(s):
        wait_halos(0, xbuf.at[s], REACH, s)
        out, conv, scale, a, t = forward(xbuf.at[s], 1, POS + 8, taps1, gain1, up1, down1)
        x1buf[...] = out.reshape(POS + 8, ROWS, C)
        near = slice(3 * ROWS, 3 * ROWS + MN)
        conv1[s] = conv[near]
        scale1[s] = scale[near]
        slope1[s] = gelu_slope(a[near], t[near])

        @pl.when(first)
        def _():
            x1buf[pl.ds(0, 4)] = jnp.zeros((4, ROWS, C), BF16)

        @pl.when(last)
        def _():
            x1buf[pl.ds(4 + POS, 4)] = jnp.zeros((4, ROWS, C), BF16)

        grad_top(s, 1, POS)
        out, conv, scale, a, t = forward(x1buf, 4, POS, taps2, gain2, up2, down2)
        x2buf[s] = out
        grad_conv = backward(gy2[pl.ds(ROWS, M)], conv, scale, gelu_slope(a, t), gain2, up2t, down2t)
        gc2buf[s, pl.ds(REACH, POS)] = grad_conv.reshape(POS, ROWS, C)
        send_halos(1, gc2buf.at[s], REACH, s)

    def stage_c(s):
        wait_halos(1, gc2buf.at[s], REACH, s)
        grad_top(s, 0, NEAR)
        grad = spread(gy2[...], gc2buf.at[s], 4, NEAR, taps2)
        grad_conv = backward(grad, conv1[s], scale1[s], slope1[s], gain1, up1t, down1t)
        gc1buf[...] = grad_conv.reshape(NEAR, ROWS, C)

        @pl.when(first)
        def _():
            gc1buf[0] = jnp.zeros((ROWS, C), BF16)

        @pl.when(last)
        def _():
            gc1buf[NEAR - 1] = jnp.zeros((ROWS, C), BF16)

        result = spread(grad[ROWS : ROWS + M], gc1buf, 1, POS, taps1)
        obuf[s] = result.astype(BF16).reshape(POS, ROWS, C)
        for step in range(1, POS):
            o_send((me + step) % POS, s).start()
        o_local(s).start()

    def pool_first():
        def pick(r):
            def match(row, col):
                j, place, bin_ = row % 16, col % M, col % ROWS
                return jnp.logical_and(
                    jnp.logical_and(row // 16 == place // ROWS, j // 4 == col // M), 4 * (j % 4) + r == bin_
                )

            return one_hot((M, SUB * M), match)

        x2_all = x2buf[...].reshape(SUB * M, C)
        for r in range(4):
            xsel[r] = dot(pick(r), x2_all)
        midb[...] = (pool1[0:1] * xsel[1] + pool1[1:2] * xsel[2] + pool1[2:3] * xsel[3]).astype(BF16)
        last_x = one_hot((16, M), lambda row, col: jnp.logical_and(col == row * 16 + 15, row < POS))
        last_m = one_hot((16, M), lambda row, col: col == (row - POS) * 16 + 15)
        rimbuf[...] = (dot(last_x, xsel[3].astype(BF16)) + dot(last_m, midb[...])).astype(BF16)
        remote(rimbuf, rim_a, rs.at[2], rr.at[2], follow).start()
        pl.when(has_over)(lambda: remote(rimbuf, rim_b, rs.at[3], rr.at[3], over).start())

    def pool_second():
        remote(rimbuf, rim_a, rs.at[2], rr.at[2], follow).wait_recv()
        pl.when(has_under)(lambda: remote(rimbuf, rim_b, rs.at[3], rr.at[3], under).wait_recv())
        shift = jnp.where(head, 1, 0)
        step_back = one_hot((M, M), lambda row, col: jnp.logical_and(row % 16 != 0, col == row - 1))

        def rim_of(base):
            def from_a(row, col):
                k = row // 16 - shift
                return jnp.logical_and(row % 16 == 0, jnp.logical_and(k >= 0, col == base + k))

            def from_b(row, col):
                return jnp.logical_and(row == 0, col == base + POS - 1)

            return dot(one_hot((M, 16), from_a), rim_a[...]) + dot(one_hot((M, 16), from_b), rim_b[...])

        x_back = dot(step_back, xsel[3].astype(BF16)) + rim_of(0)
        mid_back = dot(step_back, midb[...]) + rim_of(POS)
        mid_even = (pool1[0:1] * x_back + pool1[1:2] * xsel[0] + pool1[2:3] * xsel[1]).astype(BF16)
        pooled = pool2[0:1] * mid_back + pool2[1:2] * mid_even.astype(F32) + pool2[2:3] * midb[...].astype(F32)
        pbuf[...] = pooled.astype(BF16).reshape(POS, 16, C)
        for step in range(1, POS):
            p_send((me + step) % POS).start()
        p_local().start()

    def pipeline(t, carry):
        pl.when(t < SUB)(lambda: stage_a(t))
        pl.when(t == 1)(take_g)
        pl.when(t == 2)(share_g)
        pl.when(t == SUB)(take_g_rims)
        pl.when(jnp.logical_and(t >= 1, t <= SUB))(lambda: stage_b(t - 1))
        pl.when(t == SUB + 1)(pool_second)
        pl.when(t >= 2)(lambda: stage_c(t - 2))
        pl.when(t == SUB)(pool_first)
        return carry

    lax.fori_loop(0, SUB + 2, pipeline, 0)

    for step in range(1, POS):
        j = (me + step) % POS
        g_send(j).wait_send()
        p_send(j).wait_send()
        p_recv(j).wait_recv()
    p_local().wait()

    def drain(s, carry):
        for step in range(1, POS):
            j = (me + step) % POS
            x_send(j, s).wait_send()
            o_send(j, s).wait_send()
            o_recv(j, s).wait_recv()
        o_local(s).wait()
        end_halos(0, xbuf.at[s], REACH, s)
        end_halos(1, gc2buf.at[s], REACH, s)
        return carry

    lax.fori_loop(0, SUB, drain, 0)
    end_halos(2, gbuf, 1, 0)
    remote(grimbuf, grim_a, rs.at[0], rr.at[0], before).wait_send()
    remote(rimbuf, rim_a, rs.at[2], rr.at[2], follow).wait_send()
    pl.when(has_under)(lambda: remote(grimbuf, grim_b, rs.at[1], rr.at[1], under).wait_send())
    pl.when(has_over)(lambda: remote(rimbuf, rim_b, rs.at[3], rr.at[3], over).wait_send())


def body(
    sequence_input, first_depthwise_taps, first_norm_gain, first_up_weight, first_down_weight,
    second_depthwise_taps, second_norm_gain, second_up_weight, second_down_weight,
    pool_one, pool_two, pooled_cotangent,
):
    there = pl.BlockSpec(memory_space=pl.ANY)
    dma = pltpu.SemaphoreType.DMA
    rim = pltpu.VMEM((16, C), BF16)
    three, one = pltpu.VMEM((3, C), F32), pltpu.VMEM((1, C), F32)
    return pl.pallas_call(
        kernel,
        out_shape=(
            jax.ShapeDtypeStruct(pooled_cotangent.shape, BF16),
            jax.ShapeDtypeStruct(sequence_input.shape, BF16),
        ),
        in_specs=[there] * 12,
        out_specs=(there, there),
        scratch_shapes=[
            pltpu.VMEM((SUB, WIDE, ROWS, C), BF16),
            pltpu.VMEM((POS + 8, ROWS, C), BF16),
            pltpu.VMEM((SUB, WIDE, ROWS, C), BF16),
            pltpu.VMEM((NEAR, ROWS, C), BF16),
            pltpu.VMEM((NEAR, 16, C), BF16),
            rim, rim, rim, rim, rim, rim,
            pltpu.VMEM((SUB, MN, C), F32),
            pltpu.VMEM((SUB, MN, 1), F32),
            pltpu.VMEM((SUB, MN, HID), F32),
            pltpu.VMEM((MN, C), F32),
            pltpu.VMEM((SUB, M, C), BF16),
            pltpu.VMEM((SUB, POS, ROWS, C), BF16),
            pltpu.VMEM((POS, 16, C), BF16),
            pltpu.VMEM((4, M, C), F32),
            pltpu.VMEM((M, C), BF16),
            three, one, pltpu.VMEM((C, HID), BF16), pltpu.VMEM((HID, C), BF16),
            three, one, pltpu.VMEM((C, HID), BF16), pltpu.VMEM((HID, C), BF16),
            three, three,
            pltpu.VMEM((HID, C), BF16), pltpu.VMEM((C, HID), BF16),
            pltpu.VMEM((HID, C), BF16), pltpu.VMEM((C, HID), BF16),
            dma((SUB, POS)), dma((SUB, POS)),
            dma((POS,)), dma((POS,)),
            dma((3, SUB, 2)), dma((3, SUB, 2)),
            dma((SUB, POS)), dma((SUB, POS)),
            dma((POS,)), dma((POS,)),
            dma((4,)), dma((4,)),
            dma((10,)),
        ],
        compiler_params=pltpu.CompilerParams(
            collective_id=0, has_side_effects=True, vmem_limit_bytes=VMEM_BYTES
        ),
        cost_estimate=pl.CostEstimate(flops=4300000000, bytes_accessed=8000000, transcendentals=1000000),
    )(
        sequence_input, first_depthwise_taps, first_norm_gain.reshape(1, C), first_up_weight, first_down_weight,
        second_depthwise_taps, second_norm_gain.reshape(1, C), second_up_weight, second_down_weight,
        pool_one, pool_two, pooled_cotangent,
    )


def solution(mesh):
    split = P(None, ("major", "minor"), None)
    return jax.shard_map(
        body,
        mesh=mesh,
        in_specs=(split,) + (P(),) * 10 + (split,),
        out_specs=(split, split),
        check_vma=False,
    )
```

```python
import jax
import jax.numpy as jnp
from jax import lax
from jax.experimental import pallas as pl
from jax.experimental.pallas import tpu as pltpu
from jax.sharding import PartitionSpec as P

MESH = pl.DeviceIdType.MESH
F32 = jnp.float32
BF16 = jnp.bfloat16

C = 512
HID = 1024
MAJOR = 32
POS = 8
SUB = 4
ROWS = 16
CHUNK = SUB * ROWS
M = POS * ROWS
REACH = 5
WIDE = POS + 2 * REACH
NEAR = POS + 2
MN = NEAR * ROWS
VMEM_BYTES = 60 * 2**20
GELU_A = 0.7978845608028654
GELU_B = 0.044715


def dot(left, right):
    return jnp.dot(left, right, preferred_element_type=F32)


def one_hot(shape, match):
    row = lax.broadcasted_iota(jnp.int32, shape, 0)
    col = lax.broadcasted_iota(jnp.int32, shape, 1)
    return match(row, col).astype(F32).astype(BF16)


def rows_of(value):
    return value.reshape(-1, C)


def gelu_tanh(a):
    return jnp.tanh(GELU_A * a * (1.0 + GELU_B * (a * a)))


def gelu_slope(a, t):
    return 0.5 + 0.5 * t + 0.5 * a * (1.0 - t * t) * (GELU_A * (1.0 + 3.0 * GELU_B * (a * a)))


def kernel(
    x_ref, taps1_hbm, gain1_hbm, up1_hbm, down1_hbm, taps2_hbm, gain2_hbm, up2_hbm, down2_hbm, pool1_hbm, pool2_hbm, g_ref,
    pooled_ref, out_ref,
    xbuf, x1buf, gc2buf, gc1buf, gbuf, grimbuf, grim_a, grim_b, rimbuf, rim_a, rim_b,
    conv1, scale1, slope1, gy2, x2buf, obuf, pbuf, xsel, midb,
    taps1, gain1, up1, down1, taps2, gain2, up2, down2, pool1, pool2, up1t, down1t, up2t, down2t,
    xs, xr, gs, gr, hs, hr, os, orr, ps, pr, rs, rr, ws,
):
    major, minor = lax.axis_index("major"), lax.axis_index("minor")
    zhi, x = minor // 4, minor % 4
    half, low = x // 2, x % 2
    me = zhi * 2 + half
    first, last = major == 0, major == MAJOR - 1
    head, tail = x == 0, x == 3

    def member(j):
        return (major, (j // 2) * 4 + (j % 2) * 2 + low)

    below, above = (major - 1, minor), (major + 1, minor)
    next_x = jnp.where(half == 0, x + 2, 1 - low)
    prev_x = jnp.where(half == 1, x - 2, 3 - low)
    follow, before = (major, zhi * 4 + next_x), (major, zhi * 4 + prev_x)
    over, under = (major + 1, zhi * 4), (major - 1, zhi * 4 + 3)
    side = (major, zhi * 4 + 3 - x)

    barrier = pltpu.get_barrier_semaphore()

    def greet(device):
        pl.semaphore_signal(barrier, inc=1, device_id=device, device_id_type=MESH)

    for step in range(1, POS):
        greet(member((me + step) % POS))
    greet(side)
    pl.when(jnp.logical_not(first))(lambda: greet(below))
    pl.when(jnp.logical_not(last))(lambda: greet(above))
    pl.when(jnp.logical_and(tail, jnp.logical_not(last)))(lambda: greet(over))
    pl.when(jnp.logical_and(head, jnp.logical_not(first)))(lambda: greet(under))

    parameter_copies = [
        pltpu.make_async_copy(source, target, ws.at[k])
        for k, (source, target) in enumerate(
            (
                (taps1_hbm, taps1), (gain1_hbm, gain1), (up1_hbm, up1), (down1_hbm, down1), (taps2_hbm, taps2),
                (gain2_hbm, gain2), (up2_hbm, up2), (down2_hbm, down2), (pool1_hbm, pool1), (pool2_hbm, pool2),
            )
        )
    ]
    for copy in parameter_copies:
        copy.start()

    def remote(source, target, send, recv, device):
        return pltpu.make_async_remote_copy(
            src_ref=source, dst_ref=target, send_sem=send, recv_sem=recv,
            device_id=device, device_id_type=MESH,
        )

    def x_rows(j, s):
        return x_ref.at[j // 2, pl.ds((j % 2) * CHUNK + s * ROWS, ROWS)]

    def x_send(j, s):
        return remote(x_rows(j, s), xbuf.at[s, REACH + me], xs.at[s, j], xr.at[s, me], member(j))

    def x_recv(j, s):
        return remote(x_rows(j, s), xbuf.at[s, REACH + j], xs.at[s, j], xr.at[s, j], member(j))

    def x_local(s):
        return pltpu.make_async_copy(x_rows(me, s), xbuf.at[s, REACH + me], xr.at[s, me])

    def g_rows(j):
        return g_ref.at[j // 2, pl.ds((j % 2) * 16, 16)]

    def g_send(j):
        return remote(g_rows(j), gbuf.at[1 + me], gs.at[j], gr.at[me], member(j))

    def g_recv(j):
        return remote(g_rows(j), gbuf.at[1 + j], gs.at[j], gr.at[j], member(j))

    def g_local():
        return pltpu.make_async_copy(g_rows(me), gbuf.at[1 + me], gr.at[me])

    def out_rows(s):
        return out_ref.at[zhi, pl.ds(half * CHUNK + s * ROWS, ROWS)]

    def o_send(j, s):
        return remote(obuf.at[s, j], out_rows(s), os.at[s, j], orr.at[s, me], member(j))

    def o_recv(j, s):
        rows = out_ref.at[j // 2, pl.ds((j % 2) * CHUNK + s * ROWS, ROWS)]
        return remote(obuf.at[s, j], rows, os.at[s, j], orr.at[s, j], member(j))

    def o_local(s):
        return pltpu.make_async_copy(obuf.at[s, me], out_rows(s), orr.at[s, me])

    def p_send(j):
        rows = pooled_ref.at[zhi, pl.ds(half * 16, 16)]
        return remote(pbuf.at[j], rows, ps.at[j], pr.at[me], member(j))

    def p_recv(j):
        rows = pooled_ref.at[j // 2, pl.ds((j % 2) * 16, 16)]
        return remote(pbuf.at[j], rows, ps.at[j], pr.at[j], member(j))

    def p_local():
        return pltpu.make_async_copy(pbuf.at[me], pooled_ref.at[zhi, pl.ds(half * 16, 16)], pr.at[me])

    def halo_down(kind, buf, reach, s):
        return remote(
            buf.at[pl.ds(reach, reach)], buf.at[pl.ds(reach + POS, reach)],
            hs.at[kind, s, 0], hr.at[kind, s, 0], below,
        )

    def halo_up(kind, buf, reach, s):
        return remote(
            buf.at[pl.ds(POS, reach)], buf.at[pl.ds(0, reach)], hs.at[kind, s, 1], hr.at[kind, s, 1], above,
        )

    def send_halos(kind, buf, reach, s):
        pl.when(jnp.logical_not(first))(lambda: halo_down(kind, buf, reach, s).start())
        pl.when(jnp.logical_not(last))(lambda: halo_up(kind, buf, reach, s).start())

    def wait_halos(kind, buf, reach, s):
        pl.when(jnp.logical_not(last))(lambda: halo_down(kind, buf, reach, s).wait_recv())
        pl.when(jnp.logical_not(first))(lambda: halo_up(kind, buf, reach, s).wait_recv())

    def end_halos(kind, buf, reach, s):
        pl.when(jnp.logical_not(first))(lambda: halo_down(kind, buf, reach, s).wait_send())
        pl.when(jnp.logical_not(last))(lambda: halo_up(kind, buf, reach, s).wait_send())

    zeros = jnp.zeros((SUB, REACH, ROWS, C), BF16)

    @pl.when(first)
    def _():
        xbuf[:, pl.ds(0, REACH)] = zeros
        gc2buf[:, pl.ds(0, REACH)] = zeros
        gbuf[0] = zeros[0, 0]

    @pl.when(last)
    def _():
        xbuf[:, pl.ds(REACH + POS, REACH)] = zeros
        gc2buf[:, pl.ds(REACH + POS, REACH)] = zeros
        gbuf[1 + POS] = zeros[0, 0]

    has_under = jnp.logical_and(head, jnp.logical_not(first))
    has_over = jnp.logical_and(tail, jnp.logical_not(last))

    @pl.when(jnp.logical_not(has_under))
    def _():
        rim_b[...] = jnp.zeros((16, C), BF16)

    @pl.when(jnp.logical_not(has_over))
    def _():
        grim_b[...] = jnp.zeros((16, C), BF16)

    partners = (
        POS
        + jnp.where(first, 0, 1) + jnp.where(last, 0, 1)
        + jnp.where(has_over, 1, 0) + jnp.where(has_under, 1, 0)
    )
    pl.semaphore_wait(barrier, partners)

    def send_x(s):
        for step in range(1, POS):
            x_send((me + step) % POS, s).start()
        x_local(s).start()

    def send_g():
        for step in range(1, POS):
            g_send((me + step) % POS).start()
        g_local().start()

    send_x(0)
    send_x(1)
    send_g()
    send_x(2)

    for copy in parameter_copies:
        copy.wait()
    up1t[...] = up1[...].T
    down1t[...] = down1[...].T
    up2t[...] = up2[...].T
    down2t[...] = down2[...].T

    def three_of(buf, reach, count):
        return [rows_of(buf[pl.ds(k * reach, count)]).astype(F32) for k in range(3)]

    def forward(buf, reach, count, taps, gain, up, down):
        lowered, here, raised = three_of(buf, reach, count)
        conv = taps[0:1] * lowered + taps[1:2] * here + taps[2:3] * raised
        scale = lax.rsqrt(jnp.mean(conv * conv, -1, keepdims=True) + 1e-06)
        normed = (conv * scale * gain[...]).astype(BF16)
        a = dot(normed, up[...])
        t = gelu_tanh(a)
        hidden = (a * (0.5 + 0.5 * t)).astype(BF16)
        out = (here + dot(hidden, down[...])).astype(BF16)
        return out, conv, scale, a, t

    def backward(grad, conv, scale, slope, gain, upt, downt):
        grad_pre = (slope * dot(grad.astype(BF16), downt[...])).astype(BF16)
        scaled = dot(grad_pre, upt[...]) * gain[...]
        mean = jnp.mean(scaled * conv, -1, keepdims=True)
        return (scale * scaled - conv * (scale * scale * scale) * mean).astype(BF16)

    def spread(grad, buf, reach, count, taps):
        lowered, here, raised = three_of(buf, reach, count)
        return grad + taps[0:1] * raised + taps[1:2] * here + taps[2:3] * lowered

    def top_coefficients(rows):
        one, two = [pool1[k : k + 1] for k in range(3)], [pool2[k : k + 1] for k in range(3)]
        here = (one[1] * two[1], one[2] * two[1] + one[0] * two[2], one[1] * two[2], one[2] * two[2])
        ahead = (jnp.zeros((1, C), F32), one[0] * two[0], one[1] * two[0], one[2] * two[0] + one[0] * two[1])
        place = lax.broadcasted_iota(jnp.int32, (rows, C), 0) % 4

        def pick(four):
            return jnp.where(place == 0, four[0], jnp.where(place == 1, four[1], jnp.where(place == 2, four[2], four[3])))

        return pick(here), pick(ahead)

    def take_g():
        for step in range(1, POS):
            g_recv((me + step) % POS).wait_recv()
        g_local().wait()
        send_halos(2, gbuf, 1, 0)

    def share_g():
        wait_halos(2, gbuf, 1, 0)
        firsts = one_hot((16, MN), lambda row, col: jnp.logical_and(col == row * 16, row < NEAR))
        grimbuf[...] = dot(firsts, rows_of(gbuf[...])).astype(BF16)
        remote(grimbuf, grim_a, rs.at[0], rr.at[0], before).start()
        pl.when(has_under)(lambda: remote(grimbuf, grim_b, rs.at[1], rr.at[1], under).start())

    def take_g_rims():
        remote(grimbuf, grim_a, rs.at[0], rr.at[0], before).wait_recv()
        pl.when(has_over)(lambda: remote(grimbuf, grim_b, rs.at[1], rr.at[1], over).wait_recv())

    def grad_top(s, start, count):
        rows = count * ROWS
        place = pl.ds(start * ROWS, rows)
        coef_here, coef_ahead = top_coefficients(rows)
        g_all = rows_of(gbuf[pl.ds(start, count)])

        def take(row, col, ahead):
            return jnp.logical_and(row // ROWS == col // 16, (row % ROWS) // 4 + ahead + 4 * s == col % 16)

        here = dot(one_hot((rows, rows), lambda row, col: take(row, col, 0)), g_all)
        ahead = dot(one_hot((rows, rows), lambda row, col: take(row, col, 1)), g_all)
        gy2[place] = coef_here * here + coef_ahead * ahead

        @pl.when(s == SUB - 1)
        def _():
            shift = jnp.where(tail, 1, 0)

            def end(row):
                return row % ROWS >= ROWS - 4

            def from_a(row, col):
                return jnp.logical_and(end(row), jnp.logical_and(row // ROWS + start + shift == col, col < NEAR))

            def from_b(row, col):
                return jnp.logical_and(end(row), jnp.logical_and(row // ROWS + start == NEAR - 1, col == 2))

            rim = dot(one_hot((rows, 16), from_a), grim_a[...]) + dot(one_hot((rows, 16), from_b), grim_b[...])
            gy2[place] = gy2[place] + coef_ahead * rim

    def stage_a(s):
        for step in range(1, POS):
            x_recv((me + step) % POS, s).wait_recv()
        x_local(s).wait()
        send_halos(0, xbuf.at[s], REACH, s)

    def stage_b(s):
        wait_halos(0, xbuf.at[s], REACH, s)
        out, conv, scale, a, t = forward(xbuf.at[s], 1, POS + 8, taps1, gain1, up1, down1)
        x1buf[...] = out.reshape(POS + 8, ROWS, C)
        near = slice(3 * ROWS, 3 * ROWS + MN)
        conv1[s] = conv[near]
        scale1[s] = scale[near]
        slope1[s] = gelu_slope(a[near], t[near])

        @pl.when(first)
        def _():
            x1buf[pl.ds(0, 4)] = jnp.zeros((4, ROWS, C), BF16)

        @pl.when(last)
        def _():
            x1buf[pl.ds(4 + POS, 4)] = jnp.zeros((4, ROWS, C), BF16)

        grad_top(s, 1, POS)
        out, conv, scale, a, t = forward(x1buf, 4, POS, taps2, gain2, up2, down2)
        x2buf[s] = out
        grad_conv = backward(gy2[pl.ds(ROWS, M)], conv, scale, gelu_slope(a, t), gain2, up2t, down2t)
        gc2buf[s, pl.ds(REACH, POS)] = grad_conv.reshape(POS, ROWS, C)
        send_halos(1, gc2buf.at[s], REACH, s)

    def stage_c(s):
        wait_halos(1, gc2buf.at[s], REACH, s)
        grad_top(s, 0, NEAR)
        grad = spread(gy2[...], gc2buf.at[s], 4, NEAR, taps2)
        grad_conv = backward(grad, conv1[s], scale1[s], slope1[s], gain1, up1t, down1t)
        gc1buf[...] = grad_conv.reshape(NEAR, ROWS, C)

        @pl.when(first)
        def _():
            gc1buf[0] = jnp.zeros((ROWS, C), BF16)

        @pl.when(last)
        def _():
            gc1buf[NEAR - 1] = jnp.zeros((ROWS, C), BF16)

        result = spread(grad[ROWS : ROWS + M], gc1buf, 1, POS, taps1)
        obuf[s] = result.astype(BF16).reshape(POS, ROWS, C)
        for step in range(1, POS):
            o_send((me + step) % POS, s).start()
        o_local(s).start()

    def pool_first():
        def pick(r):
            def match(row, col):
                j, place, bin_ = row % 16, col % M, col % ROWS
                return jnp.logical_and(
                    jnp.logical_and(row // 16 == place // ROWS, j // 4 == col // M), 4 * (j % 4) + r == bin_
                )

            return one_hot((M, SUB * M), match)

        x2_all = x2buf[...].reshape(SUB * M, C)
        for r in range(4):
            xsel[r] = dot(pick(r), x2_all)
        midb[...] = (pool1[0:1] * xsel[1] + pool1[1:2] * xsel[2] + pool1[2:3] * xsel[3]).astype(BF16)
        last_x = one_hot((16, M), lambda row, col: jnp.logical_and(col == row * 16 + 15, row < POS))
        last_m = one_hot((16, M), lambda row, col: col == (row - POS) * 16 + 15)
        rimbuf[...] = (dot(last_x, xsel[3].astype(BF16)) + dot(last_m, midb[...])).astype(BF16)
        remote(rimbuf, rim_a, rs.at[2], rr.at[2], follow).start()
        pl.when(has_over)(lambda: remote(rimbuf, rim_b, rs.at[3], rr.at[3], over).start())

    def pool_second():
        remote(rimbuf, rim_a, rs.at[2], rr.at[2], follow).wait_recv()
        pl.when(has_under)(lambda: remote(rimbuf, rim_b, rs.at[3], rr.at[3], under).wait_recv())
        shift = jnp.where(head, 1, 0)
        step_back = one_hot((M, M), lambda row, col: jnp.logical_and(row % 16 != 0, col == row - 1))

        def rim_of(base):
            def from_a(row, col):
                k = row // 16 - shift
                return jnp.logical_and(row % 16 == 0, jnp.logical_and(k >= 0, col == base + k))

            def from_b(row, col):
                return jnp.logical_and(row == 0, col == base + POS - 1)

            return dot(one_hot((M, 16), from_a), rim_a[...]) + dot(one_hot((M, 16), from_b), rim_b[...])

        x_back = dot(step_back, xsel[3].astype(BF16)) + rim_of(0)
        mid_back = dot(step_back, midb[...]) + rim_of(POS)
        mid_even = (pool1[0:1] * x_back + pool1[1:2] * xsel[0] + pool1[2:3] * xsel[1]).astype(BF16)
        pooled = pool2[0:1] * mid_back + pool2[1:2] * mid_even.astype(F32) + pool2[2:3] * midb[...].astype(F32)
        pbuf[...] = pooled.astype(BF16).reshape(POS, 16, C)
        for step in range(1, POS):
            p_send((me + step) % POS).start()
        p_local().start()

    def pipeline(t, carry):
        pl.when(t < SUB)(lambda: stage_a(t))
        pl.when(t == 0)(lambda: send_x(3))
        pl.when(t == 1)(take_g)
        pl.when(t == 2)(share_g)
        pl.when(t == SUB)(take_g_rims)
        pl.when(jnp.logical_and(t >= 1, t <= SUB))(lambda: stage_b(t - 1))
        pl.when(t == SUB + 1)(pool_second)
        pl.when(t >= 2)(lambda: stage_c(t - 2))
        pl.when(t == SUB)(pool_first)
        return carry

    lax.fori_loop(0, SUB + 2, pipeline, 0)

    for step in range(1, POS):
        j = (me + step) % POS
        g_send(j).wait_send()
        p_send(j).wait_send()
        p_recv(j).wait_recv()
    p_local().wait()

    def drain(s, carry):
        for step in range(1, POS):
            j = (me + step) % POS
            x_send(j, s).wait_send()
            o_send(j, s).wait_send()
            o_recv(j, s).wait_recv()
        o_local(s).wait()
        end_halos(0, xbuf.at[s], REACH, s)
        end_halos(1, gc2buf.at[s], REACH, s)
        return carry

    lax.fori_loop(0, SUB, drain, 0)
    end_halos(2, gbuf, 1, 0)
    remote(grimbuf, grim_a, rs.at[0], rr.at[0], before).wait_send()
    remote(rimbuf, rim_a, rs.at[2], rr.at[2], follow).wait_send()
    pl.when(has_under)(lambda: remote(grimbuf, grim_b, rs.at[1], rr.at[1], under).wait_send())
    pl.when(has_over)(lambda: remote(rimbuf, rim_b, rs.at[3], rr.at[3], over).wait_send())


def body(
    sequence_input, first_depthwise_taps, first_norm_gain, first_up_weight, first_down_weight,
    second_depthwise_taps, second_norm_gain, second_up_weight, second_down_weight,
    pool_one, pool_two, pooled_cotangent,
):
    there = pl.BlockSpec(memory_space=pl.ANY)
    dma = pltpu.SemaphoreType.DMA
    rim = pltpu.VMEM((16, C), BF16)
    three, one = pltpu.VMEM((3, C), F32), pltpu.VMEM((1, C), F32)
    return pl.pallas_call(
        kernel,
        out_shape=(
            jax.ShapeDtypeStruct(pooled_cotangent.shape, BF16),
            jax.ShapeDtypeStruct(sequence_input.shape, BF16),
        ),
        in_specs=[there] * 12,
        out_specs=(there, there),
        scratch_shapes=[
            pltpu.VMEM((SUB, WIDE, ROWS, C), BF16),
            pltpu.VMEM((POS + 8, ROWS, C), BF16),
            pltpu.VMEM((SUB, WIDE, ROWS, C), BF16),
            pltpu.VMEM((NEAR, ROWS, C), BF16),
            pltpu.VMEM((NEAR, 16, C), BF16),
            rim, rim, rim, rim, rim, rim,
            pltpu.VMEM((SUB, MN, C), F32),
            pltpu.VMEM((SUB, MN, 1), F32),
            pltpu.VMEM((SUB, MN, HID), F32),
            pltpu.VMEM((MN, C), F32),
            pltpu.VMEM((SUB, M, C), BF16),
            pltpu.VMEM((SUB, POS, ROWS, C), BF16),
            pltpu.VMEM((POS, 16, C), BF16),
            pltpu.VMEM((4, M, C), F32),
            pltpu.VMEM((M, C), BF16),
            three, one, pltpu.VMEM((C, HID), BF16), pltpu.VMEM((HID, C), BF16),
            three, one, pltpu.VMEM((C, HID), BF16), pltpu.VMEM((HID, C), BF16),
            three, three,
            pltpu.VMEM((HID, C), BF16), pltpu.VMEM((C, HID), BF16),
            pltpu.VMEM((HID, C), BF16), pltpu.VMEM((C, HID), BF16),
            dma((SUB, POS)), dma((SUB, POS)),
            dma((POS,)), dma((POS,)),
            dma((3, SUB, 2)), dma((3, SUB, 2)),
            dma((SUB, POS)), dma((SUB, POS)),
            dma((POS,)), dma((POS,)),
            dma((4,)), dma((4,)),
            dma((10,)),
        ],
        compiler_params=pltpu.CompilerParams(
            collective_id=0, has_side_effects=True, vmem_limit_bytes=VMEM_BYTES
        ),
        cost_estimate=pl.CostEstimate(flops=4300000000, bytes_accessed=8000000, transcendentals=1000000),
    )(
        sequence_input, first_depthwise_taps, first_norm_gain.reshape(1, C), first_up_weight, first_down_weight,
        second_depthwise_taps, second_norm_gain.reshape(1, C), second_up_weight, second_down_weight,
        pool_one, pool_two, pooled_cotangent,
    )


def solution(mesh):
    split = P(None, ("major", "minor"), None)
    return jax.shard_map(
        body,
        mesh=mesh,
        in_specs=(split,) + (P(),) * 10 + (split,),
        out_specs=(split, split),
        check_vma=False,
    )
```
